256 devices in a mesh: section: 16 (over x, y_lo, core), tensor: 16 (over z, y_hi).
Axes of the slice: x: 4, y: 4 (y_hi: 2, y_lo: 2; y = y_hi * 2 + y_lo), z: 8, core: 2. Of those that a mesh axis runs over, the one named last changes fastest.
Arguments:
- fwd_input: bfloat16 [16, 256, 8192], P('section', 'tensor'), may hold values from -6 to 6
- fwd_segments: int32 [16, 256], P('section'), may hold values from 0 to 3, never falling along the last dimension, each value on 1 to 128 neighbouring positions
- norm_gain: float32 [16, 8192], P('section'), may hold values from 0.25 to 1.75
- w_query: bfloat16 [16, 8192, 4096], P('section', None, 'tensor'), may hold values from -0.0625 to 0.0625
- w_keyval: bfloat16 [16, 2, 8192, 1024], P('section', None, None, 'tensor'), may hold values from -0.0625 to 0.0625
- w_out: bfloat16 [16, 4096, 8192], P('section', 'tensor'), may hold values from -0.09375 to 0.09375
- bwd_grad: bfloat16 [16, 128, 8192], P('section', 'tensor'), may hold values from -6 to 6
- bwd_segments: int32 [16, 128], P('section'), may hold values from 0 to 3, never falling along the last dimension, each value on 1 to 64 neighbouring positions
- parked: bfloat16 [16, 128, 8192], P('section', None, 'tensor'), may hold values from -16 to 16
- parked_input: bfloat16 [16, 128, 8192], P('section', 'tensor'), may hold values from -6 to 6
Outputs:
- received_input: bfloat16 [16, 256, 8192], P('section', 'tensor')
- grad_to_prev: bfloat16 [16, 128, 8192], P('section', 'tensor')
The draws below stay inside these ranges and needn't reach their ends.
All inputs are finite; a program needn't handle non-finite values.
Results may differ from the reference program's by a relative error of at most 0.018.
Values may be sent and summed in bfloat16 or wider, within the bound.
No kernel may reach another device: no remote copies, remote signals or barrier semaphores. Data moves between devices by JAX's collectives and lax.ppermute only.
A program may use at most 128 MiB of HBM per device.

```python
import math
import jax
import jax.numpy as jnp
import numpy as np
from jax import lax

D = 8192
HD = 128
Q_DEV = 2
TF = 256
TB = 128
HEADS = 32
KV_HEADS = 8
N_SECTION = 16
N_TENSOR = 16


def draw_parked(key, part):
    key = jax.random.fold_in(key, 11)
    dims_full = (N_SECTION, TB, N_TENSOR, Q_DEV + 2, HD)
    sample = jax.random.normal(jax.random.fold_in(key, 1), dims_full, jnp.float32)
    sample = jnp.clip(sample, -16.0, 16.0)
    return sample.reshape(N_SECTION, TB, N_TENSOR * (Q_DEV + 2) * HD).astype(jnp.bfloat16)


def level_of(stream_key, dims, cuts, least, top_value):
    gain = 1.0
    for position, shards_of in cuts:
        draws = jax.random.uniform(jax.random.fold_in(jax.random.fold_in(stream_key, 6), position), (shards_of,), jnp.float32, least / len(cuts), top_value / len(cuts))
        gain = gain * jnp.repeat(jnp.exp(draws), dims[position] // shards_of).reshape((-1,) + (1,) * (len(dims) - 1 - position))
    return gain


def length_profile(count, total, most, lean):
    loads = [(1 << 20) // math.isqrt(grade ** lean) + 1 for grade in range(2, count + 1)]
    spare, given = total - most - (count - 1), [1] * (count - 1)
    while spare > 0:
        candidates = [i for i in range(count - 1) if given[i] < most]
        pool, budget = sum([loads[i] for i in candidates]), spare
        for i in candidates:
            extra = min(most - given[i], max(1, budget * loads[i] // pool), spare)
            given[i] = given[i] + extra
            spare = spare - extra
    return np.array([most] + given)


def uneven(stream_key, amount, total, limit, slope):
    if amount == 2:
        one = jax.random.randint(stream_key, (), max(1, total - limit), min(limit, total - 1) + 1)
        return jnp.stack([one, total - one])
    sizes = jnp.asarray(length_profile(amount, total, limit, slope), jnp.int32)
    twos = (amount - 1) // 2
    donor, sink = sizes[1:1 + 2 * twos:2], sizes[2:2 + 2 * twos:2]
    slack = jnp.minimum(donor - 1, limit - sink)
    moved = jax.random.randint(jax.random.fold_in(stream_key, 1), (twos,), 0, 1 << 20) % (slack + 1)
    sizes = sizes.at[1:1 + 2 * twos:2].set(donor - moved).at[2:2 + 2 * twos:2].set(sink + moved)
    return sizes[jax.random.permutation(jax.random.fold_in(stream_key, 2), amount)]


def bell_draw(stream_key, extent, width, limit, split=(), dtype=jnp.bfloat16):
    values = width * jax.random.normal(stream_key, extent, jnp.float32)
    if split:
        values = values * level_of(stream_key, extent, split, -0.22, 0.18)
    return jnp.clip(values, -limit, limit).astype(dtype)


def setup_inputs(seed: int = 0) -> dict:
    streams_of = jax.random.split(jax.random.key(seed), 11)
    fwd_input = bell_draw(streams_of[0], (N_SECTION, TF, D), 1.0, 6.0, ((0, 16), (1, 16)))
    fwd_segments = jax.vmap(lambda own: jnp.searchsorted(jnp.cumsum(uneven(own, 4, TF, TF // 2, 1)), jnp.arange(TF), side="right"))(jax.random.split(streams_of[1], N_SECTION)).reshape((N_SECTION, TF)).astype(jnp.int32)
    norm_gain = jnp.clip(1.0 + 0.15 * jax.random.normal(streams_of[2], (N_SECTION, D), jnp.float32), 0.25, 1.75)
    w_query = bell_draw(streams_of[3], (N_SECTION, D, HEADS * HD), D ** -0.5, 0.0625, ((0, 16), (2, 16)))
    w_keyval = bell_draw(streams_of[4], (N_SECTION, 2, D, KV_HEADS * HD), D ** -0.5, 0.0625, ((0, 16), (3, 16)))
    w_out = bell_draw(streams_of[5], (N_SECTION, HEADS * HD, D), (HEADS * HD) ** -0.5, 0.09375, ((0, 16), (1, 16)))
    bwd_grad = bell_draw(streams_of[6], (N_SECTION, TB, D), 1.0, 6.0, ((0, 16), (1, 16)))
    bwd_segments = jax.vmap(lambda own: jnp.searchsorted(jnp.cumsum(uneven(own, 4, TB, TB // 2, 1)), jnp.arange(TB), side="right"))(jax.random.split(streams_of[7], N_SECTION)).reshape((N_SECTION, TB)).astype(jnp.int32)
    parked = draw_parked(jax.random.fold_in(streams_of[10], 71), 0)
    parked_input = bell_draw(streams_of[9], (N_SECTION, TB, D), 1.0, 6.0, ((0, 16), (1, 16)))
    return {"fwd_input": fwd_input, "fwd_segments": fwd_segments, "norm_gain": norm_gain, "w_query": w_query, "w_keyval": w_keyval, "w_out": w_out, "bwd_grad": bwd_grad, "bwd_segments": bwd_segments, "parked": parked, "parked_input": parked_input}


EPSILON = 1e-05
NEGATIVE = -1e+30

def norm_rows(inputs, gain_vector):
    mean_square = lax.optimization_barrier(jnp.mean(inputs * inputs, axis=-1, keepdims=True))
    return inputs * lax.rsqrt(mean_square + EPSILON) * gain_vector

def visible(segment_ids):
    length = segment_ids.shape[0]
    row_index = jnp.arange(length)[:, None]
    col_index = jnp.arange(length)[None, :]
    return (col_index <= row_index) & (segment_ids[:, None] == segment_ids[None, :])

def softmax_rows(scores, allowed):
    masked = jnp.where(allowed[None], scores, NEGATIVE)
    highest = lax.optimization_barrier(jnp.max(masked, axis=-1, keepdims=True))
    weights = jnp.exp(masked - highest)
    return weights / lax.optimization_barrier(jnp.sum(weights, axis=-1, keepdims=True))

def attend_rounded(queries, keys_heads, values_heads, allowed):
    scale_factor = queries.shape[-1] ** (-0.5)
    scores = jnp.einsum('the,she->hts', queries.astype(jnp.float32), keys_heads.astype(jnp.float32)) * scale_factor
    probs = softmax_rows(scores, allowed).astype(jnp.bfloat16)
    mixed = jnp.einsum('hts,she->the', probs.astype(jnp.float32), values_heads.astype(jnp.float32))
    return mixed.astype(jnp.bfloat16)

def backward_attention(query_saved, key_saved, value_saved, allowed, grad_out):
    scale_factor = query_saved.shape[-1] ** (-0.5)
    grad_heads = grad_out.reshape(query_saved.shape)
    scores = jnp.einsum('the,se->hts', query_saved, key_saved, preferred_element_type=jnp.float32) * scale_factor
    probs = softmax_rows(scores, allowed)
    grad_probs = jnp.einsum('the,se->hts', grad_heads, value_saved, preferred_element_type=jnp.float32)
    grad_value = jnp.einsum('hts,the->se', probs, grad_heads.astype(jnp.float32), precision=lax.Precision.HIGHEST)
    row_total = lax.optimization_barrier(jnp.sum(probs * grad_probs, axis=-1, keepdims=True))
    grad_scores = probs * (grad_probs - row_total) * scale_factor
    grad_query = jnp.einsum('hts,se->the', grad_scores, key_saved.astype(jnp.float32), precision=lax.Precision.HIGHEST)
    grad_key = jnp.einsum('hts,the->se', grad_scores, query_saved.astype(jnp.float32), precision=lax.Precision.HIGHEST)
    return (grad_query.astype(jnp.bfloat16), grad_key.astype(jnp.bfloat16), grad_value.astype(jnp.bfloat16))

def section_pass(inputs):
    fwd_rows, fwd_ids, gain_vector, query_weight, keyval_weight, out_weight, grad_rows, bwd_ids, saved_block, saved_rows = inputs
    contract = (((1,), (1,)), ((), ()))
    residual = fwd_rows.astype(jnp.float32)
    normed = norm_rows(residual, gain_vector).astype(jnp.bfloat16)
    queries = jnp.dot(normed, query_weight, preferred_element_type=jnp.float32).astype(jnp.bfloat16).reshape(TF, HEADS, HD)
    keys_all = jnp.dot(normed, keyval_weight[0], preferred_element_type=jnp.float32).astype(jnp.bfloat16).reshape(TF, KV_HEADS, HD)
    values_all = jnp.dot(normed, keyval_weight[1], preferred_element_type=jnp.float32).astype(jnp.bfloat16).reshape(TF, KV_HEADS, HD)
    group_size = HEADS // KV_HEADS
    attended = attend_rounded(queries, jnp.repeat(keys_all, group_size, axis=1), jnp.repeat(values_all, group_size, axis=1), visible(fwd_ids))
    width_dev = Q_DEV * HD
    attended = attended.reshape(TF, N_TENSOR, width_dev)
    out_parts = out_weight.reshape(N_TENSOR, width_dev, D)
    summed = jnp.zeros((TF, D), jnp.float32)
    for shard in range(N_TENSOR):
        term = jnp.dot(attended[:, shard], out_parts[shard], preferred_element_type=jnp.float32)
        summed = summed + lax.optimization_barrier(term.astype(jnp.bfloat16)).astype(jnp.float32)
    produced = (residual + summed).astype(jnp.bfloat16)
    saved_heads = saved_block.reshape(TB, N_TENSOR, Q_DEV + 2, HD)
    allowed_back = visible(bwd_ids)
    query_grads = []
    key_grads = []
    value_grads = []
    for shard in range(N_TENSOR):
        grad_out = lax.dot_general(grad_rows, out_parts[shard], contract, preferred_element_type=jnp.float32).astype(jnp.bfloat16)
        query_saved = saved_heads[:, shard, :Q_DEV]
        key_saved = saved_heads[:, shard, Q_DEV]
        value_saved = saved_heads[:, shard, Q_DEV + 1]
        grad_query, grad_key, grad_value = backward_attention(query_saved, key_saved, value_saved, allowed_back, grad_out)
        query_grads.append(grad_query.reshape(TB, width_dev))
        key_grads.append(grad_key)
        value_grads.append(grad_value)
    half_width = HD // 2
    grad_normed = jnp.zeros((TB, D), jnp.float32)
    for shard in range(N_TENSOR):
        partner = shard ^ 1
        half_start = shard % 2 * half_width
        col_start = shard // 2 * HD + half_start
        pair_key = (key_grads[shard].astype(jnp.float32) + key_grads[partner].astype(jnp.float32)).astype(jnp.bfloat16)
        pair_value = (value_grads[shard].astype(jnp.float32) + value_grads[partner].astype(jnp.float32)).astype(jnp.bfloat16)
        term = lax.dot_general(query_grads[shard], query_weight[:, shard * width_dev:(shard + 1) * width_dev], contract, preferred_element_type=jnp.float32)
        term = term + lax.dot_general(pair_key[:, half_start:half_start + half_width], keyval_weight[0][:, col_start:col_start + half_width], contract, preferred_element_type=jnp.float32)
        term = term + lax.dot_general(pair_value[:, half_start:half_start + half_width], keyval_weight[1][:, col_start:col_start + half_width], contract, preferred_element_type=jnp.float32)
        grad_normed = grad_normed + lax.optimization_barrier(term.astype(jnp.bfloat16)).astype(jnp.float32)
    previous = saved_rows.astype(jnp.float32)
    _, pull_norm = jax.vjp(lambda rows_in: norm_rows(rows_in, gain_vector), previous)
    grad_norm, = pull_norm(grad_normed)
    returned = (grad_rows.astype(jnp.float32) + grad_norm).astype(jnp.bfloat16)
    return (produced, returned)

def reference(fwd_input, fwd_segments, norm_gain, w_query, w_keyval, w_out, bwd_grad, bwd_segments, parked, parked_input):
    mirror_blocks = jnp.roll(parked, N_SECTION // 2, axis=0)
    mirror_rows = jnp.roll(parked_input, N_SECTION // 2, axis=0)
    produced, returned = lax.map(section_pass, (fwd_input, fwd_segments, norm_gain, w_query, w_keyval, w_out, bwd_grad, bwd_segments, mirror_blocks, mirror_rows))
    received_input = jnp.concatenate([jnp.zeros_like(produced[:1]), produced[:-1]], axis=0)
    grad_to_prev = jnp.roll(returned, -1, axis=0)
    return (received_input, grad_to_prev)
```

```python
import jax
import jax.numpy as jnp
from jax import lax
from jax.sharding import PartitionSpec as P

HD = 128
Q_DEV = 2
RING = 8


EPSILON = 1e-05
NEGATIVE = -1e30


def along_z(x, k):
    return lax.ppermute(
        x, "tensor", [(t, (t // 2 + k) % RING * 2 + t % 2) for t in range(2 * RING)]
    )


def across(x):
    return lax.ppermute(x, "tensor", [(t, t ^ 1) for t in range(2 * RING)])


def gather_relative(own):
    a, b = {0: own}, {}
    a[7], a[1], b[0] = along_z(own, 1), along_z(own, -1), across(own)
    a[6], a[2], b[7] = along_z(a[7], 1), along_z(a[1], -1), across(a[7])
    a[5], a[3], b[2] = along_z(a[6], 1), along_z(a[2], -1), across(a[2])
    a[4], b[1], b[5] = along_z(a[5], 1), along_z(b[0], -1), across(a[5])
    b[6], b[3], b[4] = along_z(b[7], 1), along_z(b[2], -1), across(a[4])
    return [part[d] for d in range(RING) for part in (a, b)]


def add_blocks(*terms):
    total = terms[0].astype(jnp.float32)
    for term in terms[1:]:
        total = total + term.astype(jnp.float32)
    return total.astype(jnp.bfloat16)


def scatter_relative(blocks):
    a = {d: blocks[2 * d] for d in range(RING)}
    b = {d: blocks[2 * d + 1] for d in range(RING)}
    from_up, from_down, from_side = along_z(b[6], -1), along_z(b[3], 1), across(b[4])
    b[7] = add_blocks(b[7], from_up)
    b[2] = add_blocks(b[2], from_down)
    a[4] = add_blocks(a[4], from_side)
    from_up, from_down, from_side = along_z(a[4], -1), along_z(b[1], 1), across(b[5])
    a[5] = add_blocks(a[5], from_up, from_side)
    b[0] = add_blocks(b[0], from_down)
    from_up, from_down, from_side = along_z(a[5], -1), along_z(a[3], 1), across(b[2])
    a[6] = add_blocks(a[6], from_up)
    a[2] = add_blocks(a[2], from_down, from_side)
    from_up, from_down, from_side = along_z(a[6], -1), along_z(a[2], 1), across(b[7])
    a[7] = add_blocks(a[7], from_up, from_side)
    a[1] = add_blocks(a[1], from_down)
    from_up, from_down, from_side = along_z(a[7], -1), along_z(a[1], 1), across(b[0])
    return [a[0], from_up, from_down, from_side]


def to_relative(x, z, column):
    rows = x.shape[0] // (2 * RING)
    doubled = jnp.concatenate([x, x], axis=0)
    rolled = lax.dynamic_slice_in_dim(doubled, z * 2 * rows, x.shape[0], 0)
    return jnp.where(column == 0, rolled, flip_columns(rolled))


def flip_columns(x):
    rows = x.shape[0] // (2 * RING)
    pieces = x.reshape((RING, 2, rows) + x.shape[1:])
    return jnp.concatenate([pieces[:, 1:], pieces[:, :1]], axis=1).reshape(x.shape)


def norm_rows(inputs, gain_vector):
    mean_square = jnp.mean(inputs * inputs, axis=-1, keepdims=True)
    return inputs * lax.rsqrt(mean_square + EPSILON) * gain_vector


def visible(segment_ids, z, column):
    length = segment_ids.shape[0]
    order = to_relative(jnp.arange(length), z, column)
    segments = to_relative(segment_ids, z, column)
    return (order[None, :] <= order[:, None]) & (segments[:, None] == segments[None, :])


def softmax_rows(scores, allowed):
    masked = jnp.where(allowed[None], scores, NEGATIVE)
    highest = jnp.max(masked, axis=-1, keepdims=True)
    weights = jnp.exp(masked - highest)
    return weights / jnp.sum(weights, axis=-1, keepdims=True)


def attend_rounded(queries, keys_shared, values_shared, allowed):
    scale_factor = queries.shape[-1] ** (-0.5)
    scores = (
        jnp.einsum("the,se->hts", queries, keys_shared, preferred_element_type=jnp.float32)
        * scale_factor
    )
    probs = softmax_rows(scores, allowed).astype(jnp.bfloat16)
    mixed = jnp.einsum("hts,se->the", probs, values_shared, preferred_element_type=jnp.float32)
    return mixed.astype(jnp.bfloat16)


def backward_attention(query_saved, key_saved, value_saved, allowed, grad_out):
    scale_factor = query_saved.shape[-1] ** (-0.5)
    grad_heads = grad_out.reshape(query_saved.shape)
    scores = (
        jnp.einsum("the,se->hts", query_saved, key_saved, preferred_element_type=jnp.float32)
        * scale_factor
    )
    probs = softmax_rows(scores, allowed)
    grad_probs = jnp.einsum(
        "the,se->hts", grad_heads, value_saved, preferred_element_type=jnp.float32
    )
    grad_value = jnp.einsum(
        "hts,the->se", probs, grad_heads.astype(jnp.float32), precision=lax.Precision.HIGHEST
    )
    row_total = jnp.sum(probs * grad_probs, axis=-1, keepdims=True)
    grad_scores = probs * (grad_probs - row_total) * scale_factor
    grad_query = jnp.einsum(
        "hts,se->the", grad_scores, key_saved.astype(jnp.float32), precision=lax.Precision.HIGHEST
    )
    grad_key = jnp.einsum(
        "hts,the->se", grad_scores, query_saved.astype(jnp.float32), precision=lax.Precision.HIGHEST
    )
    return (
        grad_query.astype(jnp.bfloat16),
        grad_key.astype(jnp.bfloat16),
        grad_value.astype(jnp.bfloat16),
    )


def local(
    fwd_input,
    fwd_segments,
    norm_gain,
    w_query,
    w_keyval,
    w_out,
    bwd_grad,
    bwd_segments,
    parked,
    parked_input,
):
    contract = (((1,), (1,)), ((), ()))
    sections = lax.axis_size("section")
    tensor_now = lax.axis_index("tensor")
    z, column = tensor_now // 2, tensor_now % 2
    half = HD // 2
    width = Q_DEV * HD
    gain_vector = norm_gain[0]
    query_weight = w_query[0]
    out_weight = w_out[0]
    own_keyval = w_keyval[0]
    grad_rows = bwd_grad[0]
    residual = fwd_input[0].astype(jnp.float32)
    normed = norm_rows(residual, gain_vector).astype(jnp.bfloat16)

    mirror = [(s, s ^ sections // 2) for s in range(sections)]
    grads_all = jnp.concatenate(gather_relative(grad_rows), axis=0)
    normed_all = jnp.concatenate(gather_relative(normed), axis=0)
    saved_block = lax.ppermute(parked[0], "section", mirror)
    saved_rows = lax.ppermute(parked_input[0], "section", mirror)

    saved = to_relative(saved_block, z, column)
    bwd_tokens = saved.shape[0]
    saved_heads = saved.reshape(bwd_tokens, Q_DEV + 2, HD)
    grad_attended = lax.dot_general(
        grads_all, out_weight, contract, preferred_element_type=jnp.float32
    ).astype(jnp.bfloat16)
    grad_query, grad_key, grad_value = backward_attention(
        saved_heads[:, :Q_DEV],
        saved_heads[:, Q_DEV],
        saved_heads[:, Q_DEV + 1],
        visible(bwd_segments[0], z, column),
        grad_attended,
    )
    halves = jnp.concatenate([grad_key, grad_value], axis=1).reshape(bwd_tokens, 2, 2, half)
    own_half = jnp.where(column == 0, halves[:, :, 0], halves[:, :, 1])
    other_half = jnp.where(column == 0, halves[:, :, 1], halves[:, :, 0])
    partner_half = flip_columns(across(other_half.reshape(bwd_tokens, HD)))
    pair_half = add_blocks(own_half.reshape(bwd_tokens, HD), partner_half)
    term = lax.dot_general(
        grad_query.reshape(bwd_tokens, width),
        query_weight,
        contract,
        preferred_element_type=jnp.float32,
    )
    term = term + lax.dot_general(
        pair_half[:, :half], own_keyval[0], contract, preferred_element_type=jnp.float32
    )
    term = term + lax.dot_general(
        pair_half[:, half:], own_keyval[1], contract, preferred_element_type=jnp.float32
    )
    term = term.astype(jnp.bfloat16)
    rows = grad_rows.shape[0]
    bwd_parts = scatter_relative([term[i * rows : (i + 1) * rows] for i in range(2 * RING)])

    queries = jnp.dot(normed_all, query_weight, preferred_element_type=jnp.float32)
    own_key = jnp.dot(normed_all, own_keyval[0], preferred_element_type=jnp.float32)
    own_value = jnp.dot(normed_all, own_keyval[1], preferred_element_type=jnp.float32)
    own_kv = jnp.concatenate([own_key, own_value], axis=1).astype(jnp.bfloat16)
    other_kv = flip_columns(across(own_kv))
    low = jnp.where(column == 0, own_kv, other_kv)
    high = jnp.where(column == 0, other_kv, own_kv)
    fwd_tokens = queries.shape[0]
    attended = attend_rounded(
        queries.astype(jnp.bfloat16).reshape(fwd_tokens, Q_DEV, HD),
        jnp.concatenate([low[:, :half], high[:, :half]], axis=1),
        jnp.concatenate([low[:, half:], high[:, half:]], axis=1),
        visible(fwd_segments[0], z, column),
    ).reshape(fwd_tokens, width)
    shares = jnp.dot(attended, out_weight, preferred_element_type=jnp.float32).astype(jnp.bfloat16)
    rows = residual.shape[0]
    fwd_parts = scatter_relative([shares[i * rows : (i + 1) * rows] for i in range(2 * RING)])

    grad_normed = sum(part.astype(jnp.float32) for part in bwd_parts)
    previous = saved_rows.astype(jnp.float32)
    _, pull_norm = jax.vjp(lambda rows_in: norm_rows(rows_in, gain_vector), previous)
    (grad_norm,) = pull_norm(grad_normed)
    returned = (grad_rows.astype(jnp.float32) + grad_norm).astype(jnp.bfloat16)
    sent_back = lax.ppermute(
        returned, "section", [(s, (s - 1) % sections) for s in range(sections)]
    )
    produced = (residual + sum(part.astype(jnp.float32) for part in fwd_parts)).astype(
        jnp.bfloat16
    )
    received = lax.ppermute(produced, "section", [(s, s + 1) for s in range(sections - 1)])
    return (received[None], sent_back[None])


def solution(mesh):
    return jax.shard_map(
        local,
        mesh=mesh,
        in_specs=(
            P("section", "tensor", None),
            P("section", None),
            P("section", None),
            P("section", None, "tensor"),
            P("section", None, None, "tensor"),
            P("section", "tensor", None),
            P("section", "tensor", None),
            P("section", None),
            P("section", None, "tensor"),
            P("section", "tensor", None),
        ),
        out_specs=(P("section", "tensor", None), P("section", "tensor", None)),
        check_vma=False,
    )
```

```python
import jax
import jax.numpy as jnp
from jax import lax
from jax.experimental import pallas as pl
from jax.experimental.pallas import tpu as pltpu
from jax.sharding import PartitionSpec as P

HD = 128
Q_DEV = 2
RING = 8
STEPS = 8


EPSILON = 1e-05
VMEM_LIMIT = 12 * 1024 * 1024
NEGATIVE = -1e30


def along_z(x, k):
    return lax.ppermute(
        x, "tensor", [(t, (t // 2 + k) % RING * 2 + t % 2) for t in range(2 * RING)]
    )


def across(x):
    return lax.ppermute(x, "tensor", [(t, t ^ 1) for t in range(2 * RING)])


def after(value, *others):
    return lax.optimization_barrier((value, *others))[0]


def lane(move):
    last = []

    def send(x):
        x = after(x, *last)
        last[:] = [move(x)]
        return last[0]

    return send


def lanes():
    return lane(lambda x: along_z(x, 1)), lane(lambda x: along_z(x, -1)), lane(across)


def gather_relative(own, first, parked, mirror):
    up, down, side = lanes()
    a, b = {0: own}, {}
    a[7], a[1], b[0] = up(own), down(own), side(after(own, first))
    a[6], a[2], b[7] = up(a[7]), down(a[1]), side(a[7])
    a[5], a[3], b[2] = up(a[6]), down(a[2]), side(a[2])
    a[4], b[1], b[5] = up(a[5]), down(b[0]), side(a[5])
    saved = lax.ppermute(after(parked, a[5]), "section", mirror)
    a[4], b[1], b[5], saved = lax.optimization_barrier((a[4], b[1], b[5], saved))
    b[6], b[3], b[4] = up(b[7]), down(b[2]), side(a[4])
    return [part[d] for d in range(RING) for part in (a, b)], saved


def z_groups():
    return [[2 * z + column for z in range(RING)] for column in range(2)]


def by_column(column, own, other):
    return jnp.where(column == 0, own, other), jnp.where(column == 0, other, own)


def add_blocks(*terms):
    total = terms[0].astype(jnp.float32)
    for term in terms[1:]:
        total = total + term.astype(jnp.float32)
    return total.astype(jnp.bfloat16)


def onward(x, step, cross):
    sections, devices = lax.axis_size("section"), 2 * RING
    pairs = [
        (s * devices + t, (s + 1) * devices + (((t // 2 + step) % RING * 2 + t % 2) ^ cross))
        for s in range(sections - 1)
        for t in range(devices)
    ]
    return lax.ppermute(x, ("section", "tensor"), pairs)


def scatter_relative(beside, blocks, residual):
    a = {d: blocks[2 * d] for d in range(RING)}
    b = {d: blocks[2 * d + 1] for d in range(RING)}
    up, down, side = lanes()
    from_up, from_down, from_side = down(b[6]), up(b[3]), side(b[4])
    b[7] = add_blocks(b[7], from_up)
    b[2] = add_blocks(b[2], from_down)
    a[4] = add_blocks(a[4], from_side)
    from_up, from_down, from_side = down(a[4]), up(b[1]), side(b[5])
    a[5] = add_blocks(a[5], from_up, from_side)
    b[0] = add_blocks(b[0], from_down)
    a[0] = add_blocks(after(a[0], from_down), residual)
    from_up, from_down, from_side = down(a[5]), up(a[3]), side(b[2])
    a[6] = add_blocks(a[6], from_up)
    a[2] = add_blocks(a[2], from_down, from_side)
    from_up, from_down, from_side = down(a[6]), up(a[2]), side(b[7])
    a[7] = add_blocks(a[7], from_up, from_side)
    a[1] = add_blocks(a[1], from_down)
    last = [onward(after(b[0], from_side), 0, 1)]
    last += [onward(after(a[0], from_side), 0, 0)]
    a[7], a[1], beside = lax.optimization_barrier((a[7], a[1], beside))
    last += [onward(a[7], -1, 0), onward(a[1], 1, 0)]
    return last, beside


def norm_rows(inputs, gain_vector):
    mean_square = jnp.mean(inputs * inputs, axis=-1, keepdims=True)
    return inputs * lax.rsqrt(mean_square + EPSILON) * gain_vector


def exact_dot(a, b, dims):
    return lax.dot_general(
        a,
        b.astype(jnp.float32),
        (dims, ((), ())),
        precision=lax.Precision.HIGHEST,
        preferred_element_type=jnp.float32,
    )


def dot_last(a, b):
    return lax.dot_general(a, b, (((1,), (1,)), ((), ())), preferred_element_type=jnp.float32)


def softmax_rows(scores, allowed):
    masked = jnp.where(allowed, scores, NEGATIVE)
    highest = jnp.max(masked, axis=-1, keepdims=True)
    weights = jnp.exp(masked - highest)
    return weights / jnp.sum(weights, axis=-1, keepdims=True)


def place(shape, axis):
    return lax.broadcasted_iota(jnp.int32, shape, axis)


def turned(row, square):
    same = place(square, 0) == place(square, 1)
    return jnp.sum(jnp.where(same, row, 0.0), axis=1, keepdims=True)


def fetch(source, target, sems, axis):
    size = source.shape[axis] // STEPS
    copies = []
    for i in range(STEPS):
        part = (slice(None), pl.ds(i * size, size)) if axis else (pl.ds(i * size, size),)
        copy = pltpu.make_async_copy(source.at[part], target.at[part], sems.at[i])
        copy.start()
        copies.append(copy)
    return copies


def chunks(width):
    size = width // STEPS
    return [slice(i * size, (i + 1) * size) for i in range(STEPS)]


def backward_kernel(
    where, grads, weight, saved, segments, grad_q, own, other, grads_near, weight_near, sems
):
    grad_copies = fetch(grads, grads_near, sems.at[0], 1)
    copies = fetch(weight, weight_near, sems.at[1], 1)
    tokens = saved.shape[0]
    square = (tokens, tokens)
    scale = HD**-0.5
    key = saved[:, Q_DEV * HD : (Q_DEV + 1) * HD]
    value = saved[:, (Q_DEV + 1) * HD :]
    ids = segments[...].astype(jnp.float32)
    allowed = (place(square, 1) <= place(square, 0)) & (turned(ids, square) == ids)
    heads = [slice(head * HD, (head + 1) * HD) for head in range(Q_DEV)]
    weights = [
        softmax_rows(dot_last(saved[:, part], key) * scale, allowed) for part in heads
    ]
    total = jnp.zeros((tokens, Q_DEV * HD), jnp.float32)
    for part, first, second in zip(chunks(grads.shape[1]), grad_copies, copies):
        first.wait()
        second.wait()
        total += dot_last(grads_near[:, part], weight_near[:, part])
    grad_out = total.astype(jnp.bfloat16)
    grad_key = jnp.zeros((tokens, HD), jnp.float32)
    grad_value = jnp.zeros((tokens, HD), jnp.float32)
    for part, probs in zip(heads, weights):
        query = saved[:, part]
        grad_head = grad_out[:, part]
        grad_probs = dot_last(grad_head, value)
        row_total = jnp.sum(probs * grad_probs, axis=-1, keepdims=True)
        grad_scores = probs * (grad_probs - row_total) * scale
        grad_value += exact_dot(probs.T, grad_head, ((1,), (0,)))
        grad_q[:, part] = exact_dot(grad_scores, key, ((1,), (0,))).astype(jnp.bfloat16)
        grad_key += exact_dot(grad_scores.T, query, ((1,), (0,)))
    half = HD // 2
    low = jnp.concatenate([grad_key[:, :half], grad_value[:, :half]], axis=1)
    high = jnp.concatenate([grad_key[:, half:], grad_value[:, half:]], axis=1)
    even = where[0] % 2 == 0
    own[...] = jnp.where(even, low, high).astype(jnp.bfloat16)
    other[...] = jnp.where(even, high, low).astype(jnp.bfloat16)


def term_kernel(
    grad_q, own, partner, w_query, w_keyval, out, query_near, keyval_near, out_near, sems
):
    query_copies = fetch(w_query, query_near, sems.at[0], 0)
    keyval_copies = fetch(w_keyval, keyval_near, sems.at[1], 1)
    pair = own[...].astype(jnp.float32) + partner[...].astype(jnp.float32)
    pair = pair.astype(jnp.bfloat16)
    writes = []
    for i, part in enumerate(chunks(out.shape[1])):
        query_copies[i].wait()
        keyval_copies[i].wait()
        term = dot_last(grad_q[...], query_near[part, :])
        term += jnp.dot(pair, keyval_near[:, part], preferred_element_type=jnp.float32)
        out_near[:, part] = term.astype(jnp.bfloat16)
        write = pltpu.make_async_copy(out_near.at[:, part], out.at[:, part], sems.at[2, i])
        write.start()
        writes.append(write)
    for write in writes:
        write.wait()


def project_kernel(*refs):
    pieces = refs[: 2 * RING]
    w_query, w_keyval, queries, keyval, query_near, keyval_near, sems = refs[2 * RING :]
    query_copies = fetch(w_query, query_near, sems.at[0], 0)
    keyval_copies = fetch(w_keyval, keyval_near, sems.at[1], 1)
    total_q = jnp.zeros(queries.shape, jnp.float32)
    total_kv = jnp.zeros(keyval.shape, jnp.float32)
    for i, part in enumerate(chunks(w_query.shape[0])):
        rows = jnp.concatenate([piece[:, part] for piece in pieces], axis=0)
        query_copies[i].wait()
        keyval_copies[i].wait()
        total_q += jnp.dot(rows, query_near[part, :], preferred_element_type=jnp.float32)
        total_kv += dot_last(rows, keyval_near[:, part])
    queries[...] = total_q.astype(jnp.bfloat16)
    keyval[...] = total_kv.astype(jnp.bfloat16)


def attend_kernel(where, queries, own, other, segments, weight, *rest):
    outs, (weight_near, sems) = rest[:-2], rest[-2:]
    copies = fetch(weight, weight_near, sems.at[0], 1)
    tokens = queries.shape[0]
    rows = tokens // (2 * RING)
    z, column = where[0] // 2, where[0] % 2

    def token(index):
        chip = (index // (2 * rows) + z) % RING
        side = (index // rows + column) % 2
        return (chip * 2 + side) * rows + index % rows

    square = (tokens, tokens)
    at_col, at_row = token(place((tokens, 1), 0)), token(place((1, tokens), 1))
    ids_row = segments[...].astype(jnp.float32)
    ids_col = turned(ids_row, square)
    of_col = jnp.sum(jnp.where(place(square, 1) == at_col, ids_row, 0.0), axis=1, keepdims=True)
    of_row = jnp.sum(jnp.where(place(square, 0) == at_row, ids_col, 0.0), axis=0, keepdims=True)
    allowed = (at_row <= at_col) & (of_row == of_col)
    theirs = jnp.concatenate(
        [other[(i ^ 1) * rows : ((i ^ 1) + 1) * rows, :] for i in range(2 * RING)], axis=0
    )
    mine = own[...]
    even = column == 0
    low = jnp.where(even, mine, theirs)
    high = jnp.where(even, theirs, mine)
    half = HD // 2
    key = jnp.concatenate([low[:, :half], high[:, :half]], axis=1)
    value = jnp.concatenate([low[:, half:], high[:, half:]], axis=1)
    mixed = []
    for head in range(Q_DEV):
        part = slice(head * HD, (head + 1) * HD)
        scores = dot_last(queries[:, part], key) * HD**-0.5
        probs = softmax_rows(scores, allowed).astype(jnp.bfloat16)
        mixed.append(
            jnp.dot(probs, value, preferred_element_type=jnp.float32).astype(jnp.bfloat16)
        )
    attended = jnp.concatenate(mixed, axis=1)
    for part, copy in zip(chunks(weight.shape[1]), copies):
        copy.wait()
        share = jnp.dot(attended, weight_near[:, part], preferred_element_type=jnp.float32)
        share = share.astype(jnp.bfloat16)
        for i, out in enumerate(outs):
            out[:, part] = share[i * rows : (i + 1) * rows]


def call(kernel, flops, size, outs, in_specs, out_specs, scratch, kind=jax.ShapeDtypeStruct):
    return pl.pallas_call(
        kernel,
        out_shape=[kind(shape, jnp.bfloat16) for shape in outs],
        in_specs=in_specs,
        out_specs=out_specs,
        scratch_shapes=[pltpu.VMEM(shape, jnp.bfloat16) for shape in scratch]
        + [pltpu.SemaphoreType.DMA((3, STEPS))],
        cost_estimate=pl.CostEstimate(flops=flops, bytes_accessed=size, transcendentals=0),
        compiler_params=pltpu.CompilerParams(vmem_limit_bytes=VMEM_LIMIT),
    )


def held():
    return pl.BlockSpec(memory_space=pltpu.VMEM)


def far():
    return pl.BlockSpec(memory_space=pltpu.HBM)


def scalars():
    return pl.BlockSpec(memory_space=pltpu.SMEM)


def local(
    fwd_input,
    fwd_segments,
    norm_gain,
    w_query,
    w_keyval,
    w_out,
    bwd_grad,
    bwd_segments,
    parked,
    parked_input,
):
    sections = lax.axis_size("section")
    tensor_now = lax.axis_index("tensor")
    column = tensor_now % 2
    width = Q_DEV * HD
    gain_vector = norm_gain[0]
    query_weight = w_query[0]
    out_weight = w_out[0]
    features = query_weight.shape[0]
    keyval_weight = jnp.swapaxes(w_keyval[0], 1, 2).reshape(HD, features)
    grad_rows = bwd_grad[0]
    residual = fwd_input[0].astype(jnp.float32)
    normed = norm_rows(residual, gain_vector).astype(jnp.bfloat16)
    fwd_rows, bwd_rows = normed.shape[0], grad_rows.shape[0]
    fwd_tokens, bwd_tokens = fwd_segments.shape[1], bwd_segments.shape[1]
    where_now = jnp.full((1,), tensor_now, jnp.int32)

    mirror = [(s, s ^ sections // 2) for s in range(sections)]
    grad_pair = jnp.concatenate(by_column(column, grad_rows, after(across(grad_rows), normed)), axis=0)
    grads_all = lax.all_gather(grad_pair, "tensor", axis=0, tiled=True, axis_index_groups=z_groups())
    pieces, saved_block = gather_relative(normed, grad_pair, parked[0], mirror)

    grad_query, own_half, other_half = call(
        backward_kernel,
        2 * bwd_tokens * features * width,
        2 * features * (width + bwd_tokens),
        [(bwd_tokens, width), (bwd_tokens, HD), (bwd_tokens, HD)],
        [scalars(), far(), far(), held(), held()],
        [held()] * 3,
        [(bwd_tokens, features), (width, features)],
    )(where_now, grads_all, out_weight, saved_block, bwd_segments)
    pieces, other_half = lax.optimization_barrier((pieces, other_half))
    partner_half = across(other_half)
    saved_rows = lax.ppermute(after(parked_input[0], other_half), "section", mirror)

    queries, own_kv = call(
        project_kernel,
        2 * fwd_tokens * features * (width + HD),
        2 * features * (width + HD + fwd_tokens),
        [(fwd_tokens, width), (fwd_tokens, HD)],
        [held()] * (2 * RING) + [far()] * 2,
        [held()] * 2,
        [(features, width), (HD, features)],
    )(*pieces, query_weight, keyval_weight)
    other_kv = across(own_kv)

    (term,) = call(
        term_kernel,
        2 * bwd_tokens * features * (width + HD),
        2 * features * (width + HD + bwd_tokens),
        [(bwd_tokens, features)],
        [held()] * 3 + [far()] * 2,
        [far()],
        [(features, width), (HD, features), (bwd_tokens, features)],
    )(grad_query, own_half, partner_half, query_weight, keyval_weight)
    pair_sums = lax.psum_scatter(
        term, "tensor", scatter_dimension=0, tiled=True, axis_index_groups=z_groups()
    )

    shares = call(
        attend_kernel,
        2 * fwd_tokens * features * width,
        2 * features * (width + fwd_tokens),
        [(fwd_rows, features)] * (2 * RING),
        [scalars()] + [held()] * 4 + [far()],
        [held()] * (2 * RING),
        [(width, features)],
        pltpu.VMEM,
    )(
        where_now,
        queries,
        own_kv,
        after(other_kv, term, saved_rows),
        fwd_segments,
        out_weight,
    )
    fwd_parts, pair_sums = scatter_relative(pair_sums, shares, residual)

    own_sum, other_sum = by_column(column, pair_sums[:bwd_rows], pair_sums[bwd_rows:])
    grad_normed = own_sum.astype(jnp.float32) + across(other_sum).astype(jnp.float32)
    previous = saved_rows.astype(jnp.float32)
    _, pull_norm = jax.vjp(lambda rows_in: norm_rows(rows_in, gain_vector), previous)
    (grad_norm,) = pull_norm(grad_normed)
    returned = (grad_rows.astype(jnp.float32) + grad_norm).astype(jnp.bfloat16)
    sent_back = lax.ppermute(
        returned, "section", [(s, (s - 1) % sections) for s in range(sections)]
    )
    received = add_blocks(*fwd_parts)
    return (received[None], sent_back[None])


def solution(mesh):
    return jax.shard_map(
        local,
        mesh=mesh,
        in_specs=(
            P("section", "tensor", None),
            P("section", None),
            P("section", None),
            P("section", None, "tensor"),
            P("section", None, None, "tensor"),
            P("section", "tensor", None),
            P("section", "tensor", None),
            P("section", None),
            P("section", None, "tensor"),
            P("section", "tensor", None),
        ),
        out_specs=(P("section", "tensor", None), P("section", "tensor", None)),
        check_vma=False,
    )
```

```python
import jax
import jax.numpy as jnp
from jax import lax
from jax.experimental import pallas as pl
from jax.experimental.pallas import tpu as pltpu
from jax.sharding import PartitionSpec as P

HD = 128
Q_DEV = 2
RING = 8
STEPS = 8


EPSILON = 1e-05
VMEM_LIMIT = 12 * 1024 * 1024
NEGATIVE = -1e30


def along_z(x, k):
    return lax.ppermute(
        x, "tensor", [(t, (t // 2 + k) % RING * 2 + t % 2) for t in range(2 * RING)]
    )


def across(x):
    return lax.ppermute(x, "tensor", [(t, t ^ 1) for t in range(2 * RING)])


def after(value, *others):
    return lax.optimization_barrier((value, *others))[0]


def lane(move):
    last = []

    def send(x):
        x = after(x, *last)
        last[:] = [move(x)]
        return last[0]

    return send


def lanes():
    return lane(lambda x: along_z(x, 1)), lane(lambda x: along_z(x, -1)), lane(across)


def gather_relative(own, first, parked, mirror):
    up, down, side = lanes()
    a, b = {0: own}, {}
    a[7], a[1], b[0] = up(own), down(own), side(after(own, first))
    a[6], a[2], b[7] = up(a[7]), down(a[1]), side(a[7])
    a[5], a[3], b[2] = up(a[6]), down(a[2]), side(a[2])
    a[4], b[1], b[5] = up(a[5]), down(b[0]), side(a[5])
    saved = lax.ppermute(after(parked, a[5]), "section", mirror)
    a[4], b[1], b[5], saved = lax.optimization_barrier((a[4], b[1], b[5], saved))
    b[6], b[3], b[4] = up(b[7]), down(b[2]), side(a[4])
    return [part[d] for d in range(RING) for part in (a, b)], saved


def z_groups():
    return [[2 * z + column for z in range(RING)] for column in range(2)]


def by_column(column, own, other):
    return jnp.where(column == 0, own, other), jnp.where(column == 0, other, own)


def add_blocks(*terms):
    total = terms[0].astype(jnp.float32)
    for term in terms[1:]:
        total = total + term.astype(jnp.float32)
    return total.astype(jnp.bfloat16)


def onward(x, step, cross):
    sections, devices = lax.axis_size("section"), 2 * RING
    pairs = [
        (s * devices + t, (s + 1) * devices + (((t // 2 + step) % RING * 2 + t % 2) ^ cross))
        for s in range(sections - 1)
        for t in range(devices)
    ]
    return lax.ppermute(x, ("section", "tensor"), pairs)


def scatter_relative(beside, blocks, residual):
    a = {d: blocks[2 * d] for d in range(RING)}
    b = {d: blocks[2 * d + 1] for d in range(RING)}
    up, down, side = lanes()
    from_up, from_down, from_side = down(b[6]), up(b[3]), side(b[4])
    b[7] = add_blocks(b[7], from_up)
    b[2] = add_blocks(b[2], from_down)
    a[4] = add_blocks(a[4], from_side)
    from_up, from_down, from_side = down(a[4]), up(b[1]), side(b[5])
    a[5] = add_blocks(a[5], from_up, from_side)
    b[0] = add_blocks(b[0], from_down)
    a[0] = add_blocks(after(a[0], from_down), residual)
    from_up, from_down, from_side = down(a[5]), up(a[3]), side(b[2])
    a[6] = add_blocks(a[6], from_up)
    a[2] = add_blocks(a[2], from_down, from_side)
    from_up, from_down = down(a[6]), up(a[2])
    from_side = side(b[7])
    first = [onward(after(b[0], from_side), 0, 1), onward(after(a[0], from_side), 0, 0)]
    a[7] = add_blocks(a[7], from_up, from_side)
    a[1] = add_blocks(a[1], from_down)
    a[7], a[1], beside = lax.optimization_barrier((a[7], a[1], beside))
    return first + [onward(a[7], -1, 0), onward(a[1], 1, 0)], beside


def norm_rows(inputs, gain_vector):
    mean_square = jnp.mean(inputs * inputs, axis=-1, keepdims=True)
    return inputs * lax.rsqrt(mean_square + EPSILON) * gain_vector


def exact_dot(a, b, dims):
    return lax.dot_general(
        a,
        b.astype(jnp.float32),
        (dims, ((), ())),
        precision=lax.Precision.HIGHEST,
        preferred_element_type=jnp.float32,
    )


def dot_last(a, b):
    return lax.dot_general(a, b, (((1,), (1,)), ((), ())), preferred_element_type=jnp.float32)


def softmax_rows(scores, allowed):
    masked = jnp.where(allowed, scores, NEGATIVE)
    highest = jnp.max(masked, axis=-1, keepdims=True)
    weights = jnp.exp(masked - highest)
    return weights / jnp.sum(weights, axis=-1, keepdims=True)


def place(shape, axis):
    return lax.broadcasted_iota(jnp.int32, shape, axis)


def turned(row, square):
    same = place(square, 0) == place(square, 1)
    return jnp.sum(jnp.where(same, row, 0.0), axis=1, keepdims=True)


def fetch(source, target, sems, axis):
    size = source.shape[axis] // STEPS
    copies = []
    for i in range(STEPS):
        part = (slice(None), pl.ds(i * size, size)) if axis else (pl.ds(i * size, size),)
        copy = pltpu.make_async_copy(source.at[part], target.at[part], sems.at[i])
        copy.start()
        copies.append(copy)
    return copies


def chunks(width):
    size = width // STEPS
    return [slice(i * size, (i + 1) * size) for i in range(STEPS)]


def backward_kernel(
    where, grads, weight, saved, segments, grad_q, own, other, grads_near, weight_near, sems
):
    grad_copies = fetch(grads, grads_near, sems.at[0], 1)
    copies = fetch(weight, weight_near, sems.at[1], 1)
    tokens = saved.shape[0]
    square = (tokens, tokens)
    scale = HD**-0.5
    key = saved[:, Q_DEV * HD : (Q_DEV + 1) * HD]
    value = saved[:, (Q_DEV + 1) * HD :]
    ids = segments[...].astype(jnp.float32)
    allowed = (place(square, 1) <= place(square, 0)) & (turned(ids, square) == ids)
    heads = [slice(head * HD, (head + 1) * HD) for head in range(Q_DEV)]
    weights = [
        softmax_rows(dot_last(saved[:, part], key) * scale, allowed) for part in heads
    ]
    total = jnp.zeros((tokens, Q_DEV * HD), jnp.float32)
    for part, first, second in zip(chunks(grads.shape[1]), grad_copies, copies):
        first.wait()
        second.wait()
        total += dot_last(grads_near[:, part], weight_near[:, part])
    grad_out = total.astype(jnp.bfloat16)
    grad_key = jnp.zeros((tokens, HD), jnp.float32)
    grad_value = jnp.zeros((tokens, HD), jnp.float32)
    for part, probs in zip(heads, weights):
        query = saved[:, part]
        grad_head = grad_out[:, part]
        grad_probs = dot_last(grad_head, value)
        row_total = jnp.sum(probs * grad_probs, axis=-1, keepdims=True)
        grad_scores = probs * (grad_probs - row_total) * scale
        grad_value += exact_dot(probs.T, grad_head, ((1,), (0,)))
        grad_q[:, part] = exact_dot(grad_scores, key, ((1,), (0,))).astype(jnp.bfloat16)
        grad_key += exact_dot(grad_scores.T, query, ((1,), (0,)))
    half = HD // 2
    low = jnp.concatenate([grad_key[:, :half], grad_value[:, :half]], axis=1)
    high = jnp.concatenate([grad_key[:, half:], grad_value[:, half:]], axis=1)
    even = where[0] % 2 == 0
    own[...] = jnp.where(even, low, high).astype(jnp.bfloat16)
    other[...] = jnp.where(even, high, low).astype(jnp.bfloat16)


def term_kernel(
    grad_q, own, partner, w_query, w_keyval, out, query_near, keyval_near, out_near, sems
):
    query_copies = fetch(w_query, query_near, sems.at[0], 0)
    keyval_copies = fetch(w_keyval, keyval_near, sems.at[1], 1)
    pair = own[...].astype(jnp.float32) + partner[...].astype(jnp.float32)
    pair = pair.astype(jnp.bfloat16)
    writes = []
    for i, part in enumerate(chunks(out.shape[1])):
        query_copies[i].wait()
        keyval_copies[i].wait()
        term = dot_last(grad_q[...], query_near[part, :])
        term += jnp.dot(pair, keyval_near[:, part], preferred_element_type=jnp.float32)
        out_near[:, part] = term.astype(jnp.bfloat16)
        write = pltpu.make_async_copy(out_near.at[:, part], out.at[:, part], sems.at[2, i])
        write.start()
        writes.append(write)
    for write in writes:
        write.wait()


def project_kernel(*refs):
    pieces = refs[: 2 * RING]
    w_query, w_keyval, queries, keyval, query_near, keyval_near, sems = refs[2 * RING :]
    query_copies = fetch(w_query, query_near, sems.at[0], 0)
    keyval_copies = fetch(w_keyval, keyval_near, sems.at[1], 1)
    total_q = jnp.zeros(queries.shape, jnp.float32)
    total_kv = jnp.zeros(keyval.shape, jnp.float32)
    for i, part in enumerate(chunks(w_query.shape[0])):
        rows = jnp.concatenate([piece[:, part] for piece in pieces], axis=0)
        query_copies[i].wait()
        keyval_copies[i].wait()
        total_q += jnp.dot(rows, query_near[part, :], preferred_element_type=jnp.float32)
        total_kv += dot_last(rows, keyval_near[:, part])
    queries[...] = total_q.astype(jnp.bfloat16)
    keyval[...] = total_kv.astype(jnp.bfloat16)


def attend_kernel(where, queries, own, other, segments, weight, *rest):
    outs, (weight_near, sems) = rest[:-2], rest[-2:]
    copies = fetch(weight, weight_near, sems.at[0], 1)
    tokens = queries.shape[0]
    rows = tokens // (2 * RING)
    z, column = where[0] // 2, where[0] % 2

    def token(index):
        chip = (index // (2 * rows) + z) % RING
        side = (index // rows + column) % 2
        return (chip * 2 + side) * rows + index % rows

    square = (tokens, tokens)
    at_col, at_row = token(place((tokens, 1), 0)), token(place((1, tokens), 1))
    ids_row = segments[...].astype(jnp.float32)
    ids_col = turned(ids_row, square)
    of_col = jnp.sum(jnp.where(place(square, 1) == at_col, ids_row, 0.0), axis=1, keepdims=True)
    of_row = jnp.sum(jnp.where(place(square, 0) == at_row, ids_col, 0.0), axis=0, keepdims=True)
    allowed = (at_row <= at_col) & (of_row == of_col)
    theirs = jnp.concatenate(
        [other[(i ^ 1) * rows : ((i ^ 1) + 1) * rows, :] for i in range(2 * RING)], axis=0
    )
    mine = own[...]
    even = column == 0
    low = jnp.where(even, mine, theirs)
    high = jnp.where(even, theirs, mine)
    half = HD // 2
    key = jnp.concatenate([low[:, :half], high[:, :half]], axis=1)
    value = jnp.concatenate([low[:, half:], high[:, half:]], axis=1)
    mixed = []
    for head in range(Q_DEV):
        part = slice(head * HD, (head + 1) * HD)
        scores = dot_last(queries[:, part], key) * HD**-0.5
        probs = softmax_rows(scores, allowed).astype(jnp.bfloat16)
        mixed.append(
            jnp.dot(probs, value, preferred_element_type=jnp.float32).astype(jnp.bfloat16)
        )
    attended = jnp.concatenate(mixed, axis=1)
    for part, copy in zip(chunks(weight.shape[1]), copies):
        copy.wait()
        share = jnp.dot(attended, weight_near[:, part], preferred_element_type=jnp.float32)
        share = share.astype(jnp.bfloat16)
        for i, out in enumerate(outs):
            out[:, part] = share[i * rows : (i + 1) * rows]


def call(kernel, flops, size, outs, in_specs, out_specs, scratch, kind=jax.ShapeDtypeStruct):
    return pl.pallas_call(
        kernel,
        out_shape=[kind(shape, jnp.bfloat16) for shape in outs],
        in_specs=in_specs,
        out_specs=out_specs,
        scratch_shapes=[pltpu.VMEM(shape, jnp.bfloat16) for shape in scratch]
        + [pltpu.SemaphoreType.DMA((3, STEPS))],
        cost_estimate=pl.CostEstimate(flops=flops, bytes_accessed=size, transcendentals=0),
        compiler_params=pltpu.CompilerParams(vmem_limit_bytes=VMEM_LIMIT),
    )


def held():
    return pl.BlockSpec(memory_space=pltpu.VMEM)


def far():
    return pl.BlockSpec(memory_space=pltpu.HBM)


def in_hbm(x):
    return pltpu.with_memory_space_constraint(x, pltpu.HBM)


def scalars():
    return pl.BlockSpec(memory_space=pltpu.SMEM)


def local(
    fwd_input,
    fwd_segments,
    norm_gain,
    w_query,
    w_keyval,
    w_out,
    bwd_grad,
    bwd_segments,
    parked,
    parked_input,
):
    sections = lax.axis_size("section")
    tensor_now = lax.axis_index("tensor")
    column = tensor_now % 2
    width = Q_DEV * HD
    gain_vector = norm_gain[0]
    query_weight = w_query[0]
    out_weight = w_out[0]
    features = query_weight.shape[0]
    keyval_weight = jnp.swapaxes(w_keyval[0], 1, 2).reshape(HD, features)
    grad_rows = bwd_grad[0]
    residual = fwd_input[0].astype(jnp.float32)
    normed = norm_rows(residual, gain_vector).astype(jnp.bfloat16)
    fwd_rows, bwd_rows = normed.shape[0], grad_rows.shape[0]
    fwd_tokens, bwd_tokens = fwd_segments.shape[1], bwd_segments.shape[1]
    where_now = jnp.full((1,), tensor_now, jnp.int32)

    mirror = [(s, s ^ sections // 2) for s in range(sections)]
    grad_pair = jnp.concatenate(by_column(column, grad_rows, after(across(grad_rows), normed)), axis=0)
    grads_all = lax.all_gather(grad_pair, "tensor", axis=0, tiled=True, axis_index_groups=z_groups())
    pieces, saved_block = gather_relative(normed, grad_pair, parked[0], mirror)

    grad_query, own_half, other_half = call(
        backward_kernel,
        2 * bwd_tokens * features * width,
        2 * features * (width + bwd_tokens),
        [(bwd_tokens, width), (bwd_tokens, HD), (bwd_tokens, HD)],
        [scalars(), far(), far(), held(), held()],
        [held()] * 3,
        [(bwd_tokens, features), (width, features)],
    )(where_now, in_hbm(grads_all), in_hbm(out_weight), saved_block, bwd_segments)
    pieces, other_half = lax.optimization_barrier((pieces, other_half))
    partner_half = across(other_half)
    saved_rows = lax.ppermute(after(parked_input[0], other_half), "section", mirror)

    queries, own_kv = call(
        project_kernel,
        2 * fwd_tokens * features * (width + HD),
        2 * features * (width + HD + fwd_tokens),
        [(fwd_tokens, width), (fwd_tokens, HD)],
        [held()] * (2 * RING) + [far()] * 2,
        [held()] * 2,
        [(features, width), (HD, features)],
    )(*pieces, query_weight, keyval_weight)
    other_kv = across(own_kv)

    (term,) = call(
        term_kernel,
        2 * bwd_tokens * features * (width + HD),
        2 * features * (width + HD + bwd_tokens),
        [(bwd_tokens, features)],
        [held()] * 3 + [far()] * 2,
        [far()],
        [(features, width), (HD, features), (bwd_tokens, features)],
    )(grad_query, own_half, partner_half, query_weight, keyval_weight)
    pair_sums = lax.psum_scatter(
        term, "tensor", scatter_dimension=0, tiled=True, axis_index_groups=z_groups()
    )

    shares = call(
        attend_kernel,
        2 * fwd_tokens * features * width,
        2 * features * (width + fwd_tokens),
        [(fwd_rows, features)] * (2 * RING),
        [scalars()] + [held()] * 4 + [far()],
        [held()] * (2 * RING),
        [(width, features)],
        pltpu.VMEM,
    )(
        where_now,
        queries,
        own_kv,
        after(other_kv, term, saved_rows),
        fwd_segments,
        in_hbm(out_weight),
    )
    fwd_parts, pair_sums = scatter_relative(pair_sums, shares, residual)

    own_sum, other_sum = by_column(column, pair_sums[:bwd_rows], pair_sums[bwd_rows:])
    grad_normed = own_sum.astype(jnp.float32) + across(other_sum).astype(jnp.float32)
    previous = saved_rows.astype(jnp.float32)
    _, pull_norm = jax.vjp(lambda rows_in: norm_rows(rows_in, gain_vector), previous)
    (grad_norm,) = pull_norm(grad_normed)
    returned = (grad_rows.astype(jnp.float32) + grad_norm).astype(jnp.bfloat16)
    sent_back = lax.ppermute(
        returned, "section", [(s, (s - 1) % sections) for s in range(sections)]
    )
    received = add_blocks(*fwd_parts)
    return (received[None], sent_back[None])


def solution(mesh):
    return jax.shard_map(
        local,
        mesh=mesh,
        in_specs=(
            P("section", "tensor", None),
            P("section", None),
            P("section", None),
            P("section", None, "tensor"),
            P("section", None, None, "tensor"),
            P("section", "tensor", None),
            P("section", "tensor", None),
            P("section", None),
            P("section", None, "tensor"),
            P("section", "tensor", None),
        ),
        out_specs=(P("section", "tensor", None), P("section", "tensor", None)),
        check_vma=False,
    )
```
